32 devices in a mesh: parts: 2 (over y), gx: 4 (over z), gy: 2 (over x), gz: 2 (over core).
Axes of the slice: x: 2, y: 2, z: 4, core: 2. Of those that a mesh axis runs over, the one named last changes fastest.
Arguments:
- volume: bfloat16 [56, 14, 56, 48], P(('parts', 'gx'), 'gy', 'gz'), parts along dimension 0, may hold values from -6 to 6
- w_qkv: bfloat16 [2, 48, 144], replicated, may hold values from -3 to 3
- w_proj: bfloat16 [2, 48, 48], replicated, may hold values from -0.875 to 0.875
- w_up: bfloat16 [2, 48, 192], replicated, may hold values from -0.875 to 0.875
- w_down: bfloat16 [2, 192, 48], replicated, may hold values from -0.4375 to 0.4375
- norm_gain: float32 [2, 2, 48], replicated, may hold values from 0.25 to 1.75
- conv_weight: bfloat16 [27, 48, 48], replicated, may hold values from -0.15625 to 0.15625
- conv_gain: float32 [48], replicated, may hold values from 0.25 to 1.75
Outputs:
- features: bfloat16 [56, 14, 56, 48], P(('parts', 'gx'), 'gy', 'gz'), parts along dimension 0
The draws below stay inside these ranges and needn't reach their ends.
There are 2 independent parts, one for each index of `parts`. The reference program is written for one: setup_inputs(seed, part) draws one part's arguments, and reference() takes and returns one part's arrays. A program takes and returns all parts, laid end to end along the dimension named above; an argument that names none is the same for every part. Nothing has to cross between parts.
All inputs are finite; a program needn't handle non-finite values.
Results may differ from the reference program's by a relative error of at most 0.039.
The reference program's roundings to bfloat16 on the way count: a program that leaves them out, or rounds other values in their place, can miss the bound.
Values may be sent and summed in bfloat16 or wider, within the bound.
A program may use at most 64 MiB of HBM per device.

```python
import jax
import jax.numpy as jnp
from jax import lax

C = 48
HEADS = 3
MLP_WIDTH = 192
WINDOW = 7
SHIFT = 3
NX = 28
NY = 14
NZ = 56


def draw_w_qkv(key, part):
    spread = C ** (-0.5)
    base = jax.random.normal(key, (2, C, 3 * C), jnp.float32) * spread
    base = jnp.clip(base, -6.0 * spread, 6.0 * spread)
    return base.astype(jnp.bfloat16)


def block_scale(rng, dims, split, smallest, high):
    level = 1.0
    for axis_at, parts in split:
        draws = jax.random.uniform(jax.random.fold_in(jax.random.fold_in(rng, 6), axis_at), (parts,), jnp.float32, smallest / len(split), high / len(split))
        level = level * jnp.repeat(jnp.exp(draws), dims[axis_at] // parts).reshape((-1,) + (1,) * (len(dims) - 1 - axis_at))
    return level


def gaussian(stream_key, shape, scale, bound, shards=(), kind=jnp.bfloat16):
    drawn = scale * jax.random.normal(stream_key, shape, jnp.float32)
    if shards:
        drawn = drawn * block_scale(stream_key, shape, shards, -0.22, 0.18)
    return jnp.clip(drawn, -bound, bound).astype(kind)


def setup_inputs(seed: int = 0, part: int = 0) -> dict:
    key_of = jax.random.split(jax.random.key(seed), 9)
    part_splits = jax.random.split(jax.random.fold_in(key_of[8], part), 9)
    return {
        "volume": gaussian(part_splits[0], (NX, NY, NZ, C), 1.0, 6.0, ((0, 4), (1, 2), (2, 2))),
        "w_qkv": draw_w_qkv(jax.random.fold_in(key_of[8], 71), part),
        "w_proj": gaussian(key_of[2], (2, C, C), C ** -0.5, 0.875),
        "w_up": gaussian(key_of[3], (2, C, MLP_WIDTH), C ** -0.5, 0.875),
        "w_down": gaussian(key_of[4], (2, MLP_WIDTH, C), MLP_WIDTH ** -0.5, 0.4375),
        "norm_gain": jnp.clip(1.0 + 0.15 * jax.random.normal(key_of[5], (2, 2, C), jnp.float32), 0.25, 1.75),
        "conv_weight": gaussian(key_of[6], (27, C, C), (27 * C) ** -0.5, 0.15625),
        "conv_gain": jnp.clip(1.0 + 0.15 * jax.random.normal(key_of[7], (C,), jnp.float32), 0.25, 1.75),
    }


def layer_norm(values, gain):
    values = values.astype(jnp.float32)
    mean = lax.optimization_barrier(jnp.mean(values, -1, keepdims=True))
    centred = values - mean
    spread = lax.optimization_barrier(jnp.mean(centred * centred, -1, keepdims=True))
    return centred * lax.rsqrt(spread + 1e-05) * gain.astype(jnp.float32)

def to_windows(values):
    sx, sy, sz = (values.shape[0], values.shape[1], values.shape[2])
    rest = values.shape[3:]
    shaped = values.reshape((sx // WINDOW, WINDOW, sy // WINDOW, WINDOW, sz // WINDOW, WINDOW) + rest)
    order = (0, 2, 4, 1, 3, 5) + tuple(range(6, 6 + len(rest)))
    return jnp.transpose(shaped, order).reshape((-1, WINDOW ** 3) + rest)

def from_windows(values, sx, sy, sz):
    width = values.shape[-1]
    shaped = values.reshape(sx // WINDOW, sy // WINDOW, sz // WINDOW, WINDOW, WINDOW, WINDOW, width)
    return jnp.transpose(shaped, (0, 3, 1, 4, 2, 5, 6)).reshape(sx, sy, sz, width)

def attend_group(items):
    qkv, labels = items
    group, count, triple = qkv.shape
    width = triple // 3
    query = qkv[..., :width].reshape(group, count, HEADS, -1).astype(jnp.float32)
    keys = qkv[..., width:2 * width].reshape(group, count, HEADS, -1).astype(jnp.float32)
    vals = qkv[..., 2 * width:].reshape(group, count, HEADS, -1).astype(jnp.float32)
    scores = jnp.einsum('gqhd,gkhd->ghqk', query, keys) * (width // HEADS) ** (-0.5)
    same = labels[:, None, :, None] == labels[:, None, None, :]
    scores = jnp.where(same, scores, -1e+30)
    scores = scores - lax.optimization_barrier(jnp.max(scores, -1, keepdims=True))
    weights = jnp.exp(scores)
    probs = (weights / lax.optimization_barrier(jnp.sum(weights, -1, keepdims=True))).astype(jnp.bfloat16)
    mixed = jnp.einsum('ghqk,gkhd->gqhd', probs.astype(jnp.float32), vals)
    return mixed.reshape(group, count, width).astype(jnp.bfloat16)

def attend(qkv, labels):
    total = qkv.shape[0]
    group = 16 if total % 16 == 0 else 1
    result = lax.map(attend_group, (qkv.reshape((total // group, group) + qkv.shape[1:]), labels.reshape(total // group, group, -1)))
    return result.reshape(total, WINDOW ** 3, -1)

def block(state, labels, w_qkv, w_proj, w_up, w_down, gains):
    sx, sy, sz, width = state.shape
    normed = layer_norm(state, gains[0]).astype(jnp.bfloat16).reshape(-1, width)
    qkv = jnp.dot(normed, w_qkv, preferred_element_type=jnp.float32).astype(jnp.bfloat16)
    qkv = qkv.reshape(sx, sy, sz, 3 * width)
    mixed = from_windows(attend(to_windows(qkv), to_windows(labels)), sx, sy, sz).reshape(-1, width)
    flat = state.reshape(-1, width).astype(jnp.float32)
    flat = (flat + jnp.dot(mixed, w_proj, preferred_element_type=jnp.float32)).astype(jnp.bfloat16)
    normed = layer_norm(flat, gains[1]).astype(jnp.bfloat16)
    upper = jax.nn.gelu(jnp.dot(normed, w_up, preferred_element_type=jnp.float32)).astype(jnp.bfloat16)
    flat = (flat.astype(jnp.float32) + jnp.dot(upper, w_down, preferred_element_type=jnp.float32)).astype(jnp.bfloat16)
    return flat.reshape(sx, sy, sz, width)

def region(coords, length):
    return jnp.where(coords < length - WINDOW, 0, jnp.where(coords < length - SHIFT, 1, 2)).astype(jnp.int32)

def make_labels(offsets, local, whole):
    lx = region(offsets[0] + jnp.arange(local[0], dtype=jnp.int32), whole[0])
    ly = region(offsets[1] + jnp.arange(local[1], dtype=jnp.int32), whole[1])
    lz = region(offsets[2] + jnp.arange(local[2], dtype=jnp.int32), whole[2])
    return 9 * lx[:, None, None] + 3 * ly[None, :, None] + lz[None, None, :]

def conv_out(centre, padded, conv_weight, conv_gain):
    sx, sy, sz, width = centre.shape
    total = jnp.zeros((sx * sy * sz, width), jnp.float32)
    for tap in range(27):
        dx, dy, dz = (tap // 9, tap // 3 % 3, tap % 3)
        piece = padded[dx:dx + sx, dy:dy + sy, dz:dz + sz].reshape(-1, width)
        total = total + jnp.dot(piece, conv_weight[tap], preferred_element_type=jnp.float32)
    active = jax.nn.leaky_relu(layer_norm(total, conv_gain), 0.01)
    return (centre.reshape(-1, width).astype(jnp.float32) + active).astype(jnp.bfloat16).reshape(sx, sy, sz, width)

def reference(volume, w_qkv, w_proj, w_up, w_down, norm_gain, conv_weight, conv_gain):
    sx, sy, sz, width = volume.shape
    plain = jnp.zeros((sx, sy, sz), jnp.int32)
    state = block(volume, plain, w_qkv[0], w_proj[0], w_up[0], w_down[0], norm_gain[0])
    state = jnp.roll(state, (-SHIFT, -SHIFT, -SHIFT), (0, 1, 2))
    labels = make_labels((0, 0, 0), (sx, sy, sz), (sx, sy, sz))
    state = block(state, labels, w_qkv[1], w_proj[1], w_up[1], w_down[1], norm_gain[1])
    state = jnp.roll(state, (SHIFT, SHIFT, SHIFT), (0, 1, 2))
    padded = jnp.pad(state, ((1, 1), (1, 1), (1, 1), (0, 0)))
    return conv_out(state, padded, conv_weight, conv_gain)
```

```python
import functools
import itertools

import jax
import jax.numpy as jnp
import numpy as np
from jax import lax
from jax.experimental import pallas as pl
from jax.experimental.pallas import tpu as pltpu
from jax.sharding import PartitionSpec as P

HEADS = 3
WINDOW = 7
SHIFT = 3
LANE = 128
TILES = 3
LANES = TILES * LANE
MESH = pl.DeviceIdType.MESH
F32 = jnp.float32
BF16 = jnp.bfloat16


def column_lanes():
    low, high = range(SHIFT), range(SHIFT, WINDOW)
    both = list(itertools.product(low, low))
    first = list(itertools.product(low, high)) + both[:6]
    second = list(itertools.product(high, low)) + both[6:]
    groups = (list(itertools.product(high, high)), first, second)
    place = {}
    for tile, group in enumerate(groups):
        for at, column in enumerate(group):
            place[column] = tile * LANE + at * WINDOW
    return place


PLACE = column_lanes()


def lane_facts():
    facts = np.zeros((8, LANES), np.int32)
    for (x, y), lane in PLACE.items():
        for z in range(WINDOW):
            facts[0, lane + z] = x < SHIFT
            facts[1, lane + z] = y < SHIFT
            facts[2, lane + z] = z < SHIFT
            facts[3, lane + z] = 1
    return facts


def norm_columns(values, gain):
    mean = jnp.mean(values, 0, keepdims=True)
    centred = values - mean
    spread = jnp.mean(centred * centred, 0, keepdims=True)
    return centred * lax.rsqrt(spread + 1e-05) * gain


def norm_rows(values, gain):
    mean = jnp.mean(values, -1, keepdims=True)
    centred = values - mean
    spread = jnp.mean(centred * centred, -1, keepdims=True)
    return centred * lax.rsqrt(spread + 1e-05) * gain


def dot(a, b):
    return jnp.dot(a, b, preferred_element_type=F32)


def block(state, key_mask, query_mask, w_qkv, w_proj, w_up, w_down, gain0, gain1):
    width = state.shape[0]
    depth = width // HEADS
    normed = norm_columns(state, gain0).astype(BF16)
    qkv = dot(w_qkv, normed)
    scale = depth ** (-0.5) * np.log2(np.e)
    query = (qkv[:width] * scale).astype(BF16)
    keys = qkv[width : 2 * width].astype(BF16)
    vals = qkv[2 * width :].astype(BF16)
    ones = jnp.ones((16, LANES), BF16)
    mixed = []
    for head in range(HEADS):
        rows = slice(head * depth, (head + 1) * depth)
        q = jnp.concatenate([query[rows], query_mask], 0)
        k = jnp.concatenate([keys[rows], key_mask], 0)
        scores = lax.dot_general(k, q, (((0,), (0,)), ((), ())), preferred_element_type=F32)
        top = jnp.max(scores, 0, keepdims=True)
        weights = jnp.exp2(scores - top).astype(BF16)
        both = dot(jnp.concatenate([vals[rows], ones], 0), weights)
        mixed.append(both[:depth] / both[depth : depth + 1])
    mixed = jnp.concatenate(mixed, 0).astype(BF16)
    state = (state + dot(w_proj, mixed)).astype(BF16).astype(F32)
    normed = norm_columns(state, gain1).astype(BF16)
    upper = jax.nn.gelu(dot(w_up, normed)).astype(BF16)
    return (state + dot(w_down, upper)).astype(BF16)


def kernel(
    sizes, facts_ref, vol_ref, wqkv_ref, wproj_ref, wup_ref, wdown_ref, gain_ref, cw_ref, cg_ref,
    out_ref, wide, win, r1, r2, tqkv, tproj, tup, tdown, tgain, rows_s, pad, cols, cw, ys,
    send1, recv1, send2, recv2,
):
    sx, sy, sz, width = sizes
    nwin = sz // WINDOW
    axes = ("gx", "gy", "gz")
    here = [lax.axis_index(a) for a in axes]
    count = [lax.axis_size(a) for a in axes]

    def device(steps, sign):
        return {
            a: lax.rem(here[i] + sign * steps[i] + count[i], count[i]) for i, a in enumerate(axes)
        }

    others = [s for s in itertools.product((0, 1), repeat=3) if any(s)]
    barrier = pltpu.get_barrier_semaphore()
    for steps in others:
        for sign in (-1, 1):
            pl.semaphore_signal(barrier, inc=1, device_id=device(steps, sign), device_id_type=MESH)

    for b in range(2):
        tqkv[b] = wqkv_ref[b].astype(F32).T.astype(BF16)
        tproj[b] = wproj_ref[b].astype(F32).T.astype(BF16)
        tup[b] = wup_ref[b].astype(F32).T.astype(BF16)
        tdown[b] = wdown_ref[b].astype(F32).T.astype(BF16)
        for i in range(2):
            wide_gain = jnp.broadcast_to(gain_ref[b, i : i + 1, :], (LANE, width)).T
            tgain[b, i] = jnp.concatenate([wide_gain] * TILES, 1)
    for dy in range(3):
        for dz in range(3):
            cw[dy, dz * width : (dz + 1) * width, :] = jnp.concatenate(
                [cw_ref[9 * dx + 3 * dy + dz].astype(F32) for dx in range(3)], 1
            ).astype(BF16)

    win[...] = jnp.zeros_like(win)
    wide[:, :sz, :] = vol_ref[...].reshape(sx * sy, sz, width).astype(F32)

    def gather(w, carry):
        for (x, y), lane in PLACE.items():
            win[w, pl.ds(lane, WINDOW), :] = wide[x * sy + y, pl.ds(w * WINDOW, WINDOW), :]
        return carry

    lax.fori_loop(0, nwin, gather, 0)

    xlow, ylow, zlow, valid = [facts_ref[i : i + 1, :] for i in range(4)]
    last = [jnp.where(here[i] == count[i] - 1, 1, 0) for i in range(3)]
    row = lax.broadcasted_iota(jnp.int32, (16, LANES), 0)

    def masks(code):
        key = jnp.where(row == 8, 1 - valid, jnp.where(row == code, valid, 0))
        query = jnp.where(row == code, 0.0, jnp.where(row <= 8, -1e30, 0.0))
        return key.astype(F32).astype(BF16), query.astype(BF16)

    def labels(w):
        edge = last[2] * jnp.where(w == nwin - 1, 1, 0)
        return masks(4 * last[0] * xlow + 2 * last[1] * ylow + edge * zlow)

    def weights(b):
        return tqkv[b], tproj[b], tup[b], tdown[b], tgain[b, 0], tgain[b, 1]

    def put(ref, at, value):
        for tile in range(TILES):
            ref[0, at, tile] = value[:, tile * LANE : (tile + 1) * LANE]

    spans = {0: (0, 1), 1: (1, 1), 2: (2, 1), 3: (1, 2)}

    def copies1(w, across):
        found = []
        for source in range(0 if across else 1, 4):
            start, size = spans[source]
            steps = (source % 2, source // 2, 1 if across else 0)
            sem = 3 * nwin + source if across else 3 * w + source - 1
            found.append(
                pltpu.make_async_remote_copy(
                    src_ref=r1.at[0, w, pl.ds(start, size)],
                    dst_ref=r1.at[source, nwin if across else w, pl.ds(start, size)],
                    send_sem=send1.at[sem],
                    recv_sem=recv1.at[sem],
                    device_id=device(steps, -1),
                    device_id_type=MESH,
                )
            )
        return found

    def copies2(w, across):
        found = []
        for source in range(0 if across else 1, 4):
            steps = (source % 2, source // 2, 1 if across else 0)
            sem = 3 * nwin + source if across else 3 * w + source - 1
            found.append(
                pltpu.make_async_remote_copy(
                    src_ref=r2.at[0, w + 1],
                    dst_ref=r2.at[source, 0 if across else w + 1],
                    send_sem=send2.at[sem],
                    recv_sem=recv2.at[sem],
                    device_id=device(steps, 1),
                    device_id_type=MESH,
                )
            )
        return found

    plain_key, plain_query = masks(jnp.zeros((1, LANES), jnp.int32))

    def first(i, carry):
        w = lax.rem(i + nwin - 1, nwin)
        out = block(win[w].T, plain_key, plain_query, *weights(0))
        put(r1, w, out)

        @pl.when(i == 0)
        def _():
            pl.semaphore_wait(barrier, 2 * len(others))

        for copy in copies1(w, False):
            copy.start()

        @pl.when(w == 0)
        def _():
            for copy in copies1(0, True):
                copy.start()

        return carry

    lax.fori_loop(0, nwin, first, 0)

    def natural1(j):
        both = (xlow * ylow) == 1
        one = both[:, LANE : 2 * LANE]
        two = both[:, 2 * LANE :]
        return jnp.concatenate(
            [
                r1[0, j, 0].astype(F32),
                jnp.where(one, r1[3, j, 1].astype(F32), r1[1, j, 1].astype(F32)),
                jnp.where(two, r1[3, j, 2].astype(F32), r1[2, j, 2].astype(F32)),
            ],
            1,
        )

    for w in range(nwin):
        for copy in copies1(w, False):
            copy.wait()
    for copy in copies1(0, True):
        copy.wait()

    def second(i, carry):
        w = lax.rem(i + nwin - 1, nwin)
        state = jnp.where(zlow == 1, natural1(w + 1), natural1(w))
        key_mask, query_mask = labels(w)
        out = block(state, key_mask, query_mask, *weights(1))
        put(r2, w + 1, out)
        for copy in copies2(w, False):
            copy.start()

        @pl.when(w == nwin - 1)
        def _():
            for copy in copies2(nwin - 1, True):
                copy.start()

        return carry

    lax.fori_loop(0, nwin, second, 0)

    for w in range(nwin):
        for copy in copies2(w, False):
            copy.wait()
    for copy in copies2(nwin - 1, True):
        copy.wait()

    py = sy + 2

    def spread(jj, carry):
        high_at = lax.rem(jj, nwin + 1)
        low_at = lax.rem(jj + nwin, nwin + 1)
        outer = jnp.where((jj == 0) | (jj == nwin + 1), 1, 0)
        above = jnp.where(here[2] < count[2] - 1, 1, 0)
        below = jnp.where(here[2] > 0, 1, 0)
        keep = jnp.where(zlow == 1, jnp.maximum(above, 1 - outer), jnp.maximum(below, 1 - outer))
        for source in range(4):
            tiles = []
            for tile in range(TILES):
                part = slice(tile * LANE, (tile + 1) * LANE)
                value = jnp.where(
                    zlow[:, part] == 1,
                    r2[source, low_at, tile].astype(F32),
                    r2[source, high_at, tile].astype(F32),
                )
                tiles.append(jnp.where(keep[:, part] == 1, value, 0.0))
            rows_s[source] = jnp.concatenate(tiles, 1).T
        for x in range(-1, sx + 1):
            for y in range(-1, sy + 1):
                ok = None
                fromx = x < SHIFT
                fromy = y < SHIFT
                for at, axis, size in ((x, 0, sx), (y, 1, sy)):
                    if at == -1:
                        test = here[axis] > 0
                    elif at == size:
                        test = here[axis] < count[axis] - 1
                    else:
                        continue
                    ok = test if ok is None else ok & test
                source = int(fromx) + 2 * int(fromy)
                lane = PLACE[x % WINDOW, y % WINDOW]
                value = rows_s[source, pl.ds(lane, WINDOW), :]
                if ok is not None:
                    value = jnp.where(ok, value, 0.0)
                pad[(x + 1) * py + y + 1, pl.ds(1 + WINDOW * jj, WINDOW), :] = value
        return carry

    lax.fori_loop(0, nwin + 2, spread, 0)

    deep = cols.shape[1]

    def stack(xp, carry):
        for y in range(py):
            at = xp * py + y
            cols[at] = jnp.concatenate(
                [pad[at, WINDOW + dz : WINDOW + dz + deep, :] for dz in range(3)], 1
            ).astype(BF16)
        total = None
        for dy in range(3):
            piece = cols[pl.ds(xp * py + dy, sy)].reshape(sy * deep, 3 * width)
            part = dot(piece, cw[dy])
            total = part if total is None else total + part
        ys[xp] = total
        return carry

    lax.fori_loop(0, sx + 2, stack, 0)

    def finish(x, carry):
        total = (
            ys[x][:, :width] + ys[x + 1][:, width : 2 * width] + ys[x + 2][:, 2 * width : 3 * width]
        )
        value = norm_rows(total, cg_ref[...])
        value = jnp.where(value >= 0, value, 0.01 * value).reshape(sy, deep, width)
        centre = pad[pl.ds((x + 1) * py + 1, sy), WINDOW + 1 : WINDOW + 1 + deep, :]
        out_ref[x] = (centre + value)[:, :sz].astype(BF16)
        return carry

    lax.fori_loop(0, sx, finish, 0)


def body(volume, w_qkv, w_proj, w_up, w_down, norm_gain, conv_weight, conv_gain):
    sx, sy, sz, width = volume.shape
    assert sx == WINDOW and sy == WINDOW and sz % WINDOW == 0
    nwin = sz // WINDOW
    hidden = w_up.shape[-1]
    deep = -(-sz // 16) * 16
    tall = -(-(WINDOW + 2 + max(deep, sz + WINDOW)) // 8) * 8
    ncopy = 3 * nwin + 4
    padded = (sx + 2) * (sy + 2)
    vmem = pl.BlockSpec(memory_space=pltpu.VMEM)
    sems = [pltpu.SemaphoreType.DMA((ncopy,))] * 4
    return pl.pallas_call(
        functools.partial(kernel, (sx, sy, sz, width)),
        out_shape=jax.ShapeDtypeStruct(volume.shape, BF16),
        in_specs=[vmem] * 9,
        out_specs=vmem,
        scratch_shapes=[
            pltpu.VMEM((sx * sy, deep, width), F32),
            pltpu.VMEM((nwin, LANES, width), F32),
            pltpu.VMEM((4, nwin + 1, TILES, width, LANE), BF16),
            pltpu.VMEM((4, nwin + 1, TILES, width, LANE), BF16),
            pltpu.VMEM((2, 3 * width, width), BF16),
            pltpu.VMEM((2, width, width), BF16),
            pltpu.VMEM((2, hidden, width), BF16),
            pltpu.VMEM((2, width, hidden), BF16),
            pltpu.VMEM((2, 2, width, LANES), F32),
            pltpu.VMEM((4, LANES, width), F32),
            pltpu.VMEM((padded, tall, width), F32),
            pltpu.VMEM((padded, deep, 3 * width), BF16),
            pltpu.VMEM((3, 3 * width, 3 * width), BF16),
            pltpu.VMEM((sx + 2, sy * deep, 3 * width), F32),
        ]
        + sems,
        compiler_params=pltpu.CompilerParams(
            collective_id=0, has_side_effects=True, vmem_limit_bytes=48 * 1024 * 1024
        ),
    )(
        jnp.asarray(lane_facts()), volume, w_qkv, w_proj, w_up, w_down, norm_gain, conv_weight,
        conv_gain.reshape(1, width),
    )


def solution(mesh):
    placed = (P(("parts", "gx"), "gy", "gz", None), P(), P(), P(), P(), P(), P(), P())
    return jax.shard_map(
        body,
        mesh=mesh,
        in_specs=placed,
        out_specs=P(("parts", "gx"), "gy", "gz", None),
        check_vma=False,
    )
```

```python
import functools
import itertools

import jax
import jax.numpy as jnp
import numpy as np
from jax import lax
from jax.experimental import pallas as pl
from jax.experimental.pallas import tpu as pltpu
from jax.sharding import PartitionSpec as P

HEADS = 3
WINDOW = 7
SHIFT = 3
LANE = 128
TILES = 3
LANES = TILES * LANE
MESH = pl.DeviceIdType.MESH
F32 = jnp.float32
BF16 = jnp.bfloat16


def column_lanes():
    low, high = range(SHIFT), range(SHIFT, WINDOW)
    both = list(itertools.product(low, low))
    first = list(itertools.product(low, high)) + both[:6]
    second = list(itertools.product(high, low)) + both[6:]
    groups = (list(itertools.product(high, high)), first, second)
    place = {}
    for tile, group in enumerate(groups):
        for at, column in enumerate(group):
            place[column] = tile * LANE + at * WINDOW
    return place


PLACE = column_lanes()


def lane_facts():
    facts = np.zeros((8, LANES), np.int32)
    for (x, y), lane in PLACE.items():
        for z in range(WINDOW):
            facts[0, lane + z] = x < SHIFT
            facts[1, lane + z] = y < SHIFT
            facts[2, lane + z] = z < SHIFT
            facts[3, lane + z] = 1
    return facts


def norm_columns(values, gain):
    mean = jnp.mean(values, 0, keepdims=True)
    centred = values - mean
    spread = jnp.mean(centred * centred, 0, keepdims=True)
    return centred * lax.rsqrt(spread + 1e-05) * gain


def norm_rows(values, gain):
    mean = jnp.mean(values, -1, keepdims=True)
    centred = values - mean
    spread = jnp.mean(centred * centred, -1, keepdims=True)
    return centred * lax.rsqrt(spread + 1e-05) * gain


def dot(a, b):
    return jnp.dot(a, b, preferred_element_type=F32)


def block(state, key_mask, query_mask, w_qkv, w_proj, w_up, w_down, gain0, gain1):
    width = state.shape[0]
    depth = width // HEADS
    normed = norm_columns(state, gain0).astype(BF16)
    qkv = dot(w_qkv, normed)
    scale = depth ** (-0.5) * np.log2(np.e)
    query = (qkv[:width] * scale).astype(BF16)
    keys = qkv[width : 2 * width].astype(BF16)
    vals = qkv[2 * width :].astype(BF16)
    ones = jnp.ones((16, LANES), BF16)
    mixed = []
    for head in range(HEADS):
        rows = slice(head * depth, (head + 1) * depth)
        q = jnp.concatenate([query[rows], query_mask], 0)
        k = jnp.concatenate([keys[rows], key_mask], 0)
        scores = lax.dot_general(k, q, (((0,), (0,)), ((), ())), preferred_element_type=F32)
        top = jnp.max(scores, 0, keepdims=True)
        weights = jnp.exp2(scores - top).astype(BF16)
        both = dot(jnp.concatenate([vals[rows], ones], 0), weights)
        mixed.append(both[:depth] / both[depth : depth + 1])
    mixed = jnp.concatenate(mixed, 0).astype(BF16)
    state = (state + dot(w_proj, mixed)).astype(BF16).astype(F32)
    normed = norm_columns(state, gain1).astype(BF16)
    upper = jax.nn.gelu(dot(w_up, normed)).astype(BF16)
    return (state + dot(w_down, upper)).astype(BF16)


def kernel(
    sizes, facts_in, vol_in, wqkv_in, wproj_in, wup_in, tdown_in, gain_in, cw_in, cg_in,
    out_ref, facts_ref, vol_ref, wqkv_ref, wproj_ref, wup_ref, tdown, gain_ref, cw_ref, cg_ref,
    wide, win, r1, r2, tqkv, tproj, tup, tgain, rows_s, pad, cols, cw, ys,
    send1, recv1, send2, recv2, loaded,
):
    pairs = (
        (vol_in, vol_ref), (wqkv_in, wqkv_ref), (wproj_in, wproj_ref), (wup_in, wup_ref),
        (gain_in, gain_ref), (tdown_in, tdown), (facts_in, facts_ref), (cg_in, cg_ref),
        (cw_in, cw_ref),
    )
    loads = [pltpu.make_async_copy(a, b, loaded.at[i]) for i, (a, b) in enumerate(pairs)]
    for load in loads:
        load.start()

    sx, sy, sz, width = sizes
    nwin = sz // WINDOW
    axes = ("gx", "gy", "gz")
    here = [lax.axis_index(a) for a in axes]
    count = [lax.axis_size(a) for a in axes]

    def device(steps, sign):
        return {
            a: lax.rem(here[i] + sign * steps[i] + count[i], count[i]) for i, a in enumerate(axes)
        }

    others = [s for s in itertools.product((0, 1), repeat=3) if any(s)]
    barrier = pltpu.get_barrier_semaphore()
    for steps in others:
        for sign in (-1, 1):
            pl.semaphore_signal(barrier, inc=1, device_id=device(steps, sign), device_id_type=MESH)

    for load in loads[1:8]:
        load.wait()
    for b in range(2):
        tqkv[b] = wqkv_ref[b].astype(F32).T.astype(BF16)
        tproj[b] = wproj_ref[b].astype(F32).T.astype(BF16)
        tup[b] = wup_ref[b].astype(F32).T.astype(BF16)
        for i in range(2):
            wide_gain = jnp.broadcast_to(gain_ref[b, i : i + 1, :], (LANE, width)).T
            tgain[b, i] = jnp.concatenate([wide_gain] * TILES, 1)
    win[...] = jnp.zeros_like(win)
    loads[0].wait()
    wide[:, :sz, :] = vol_ref[...].reshape(sx * sy, sz, width).astype(F32)

    def gather(w, carry):
        for (x, y), lane in PLACE.items():
            win[w, pl.ds(lane, WINDOW), :] = wide[x * sy + y, pl.ds(w * WINDOW, WINDOW), :]
        return carry

    lax.fori_loop(0, nwin, gather, 0)

    xlow, ylow, zlow, valid = [facts_ref[i : i + 1, :] for i in range(4)]
    last = [jnp.where(here[i] == count[i] - 1, 1, 0) for i in range(3)]
    row = lax.broadcasted_iota(jnp.int32, (16, LANES), 0)

    def masks(code):
        key = jnp.where(row == 8, 1 - valid, jnp.where(row == code, valid, 0))
        query = jnp.where(row == code, 0.0, jnp.where(row <= 8, -1e30, 0.0))
        return key.astype(F32).astype(BF16), query.astype(BF16)

    def labels(w):
        edge = last[2] * jnp.where(w == nwin - 1, 1, 0)
        return masks(4 * last[0] * xlow + 2 * last[1] * ylow + edge * zlow)

    def weights(b):
        return tqkv[b], tproj[b], tup[b], tdown[b], tgain[b, 0], tgain[b, 1]

    def put(ref, at, value):
        for tile in range(TILES):
            ref[0, at, tile] = value[:, tile * LANE : (tile + 1) * LANE]

    spans = {0: (0, 1), 1: (1, 1), 2: (2, 1), 3: (1, 2)}

    def copies1(w, across):
        found = []
        for source in range(0 if across else 1, 4):
            start, size = spans[source]
            steps = (source % 2, source // 2, 1 if across else 0)
            sem = 3 * nwin + source if across else 3 * w + source - 1
            found.append(
                pltpu.make_async_remote_copy(
                    src_ref=r1.at[0, w, pl.ds(start, size)],
                    dst_ref=r1.at[source, nwin if across else w, pl.ds(start, size)],
                    send_sem=send1.at[sem],
                    recv_sem=recv1.at[sem],
                    device_id=device(steps, -1),
                    device_id_type=MESH,
                )
            )
        return found

    def copies2(w, across):
        found = []
        for source in range(0 if across else 1, 4):
            steps = (source % 2, source // 2, 1 if across else 0)
            sem = 3 * nwin + source if across else 3 * w + source - 1
            found.append(
                pltpu.make_async_remote_copy(
                    src_ref=r2.at[0, w + 1],
                    dst_ref=r2.at[source, 0 if across else w + 1],
                    send_sem=send2.at[sem],
                    recv_sem=recv2.at[sem],
                    device_id=device(steps, 1),
                    device_id_type=MESH,
                )
            )
        return found

    plain_key, plain_query = masks(jnp.zeros((1, LANES), jnp.int32))

    def first(i, carry):
        w = lax.rem(i + nwin - 1, nwin)
        out = block(win[w].T, plain_key, plain_query, *weights(0))
        put(r1, w, out)

        @pl.when(i == 0)
        def _():
            pl.semaphore_wait(barrier, 2 * len(others))

        for copy in copies1(w, False):
            copy.start()

        @pl.when(w == 0)
        def _():
            for copy in copies1(0, True):
                copy.start()

        return carry

    lax.fori_loop(0, nwin, first, 0)

    def natural1(j):
        both = (xlow * ylow) == 1
        one = both[:, LANE : 2 * LANE]
        two = both[:, 2 * LANE :]
        return jnp.concatenate(
            [
                r1[0, j, 0].astype(F32),
                jnp.where(one, r1[3, j, 1].astype(F32), r1[1, j, 1].astype(F32)),
                jnp.where(two, r1[3, j, 2].astype(F32), r1[2, j, 2].astype(F32)),
            ],
            1,
        )

    def second(i, carry):
        w = lax.rem(i + nwin - 1, nwin)

        @pl.when(i == 0)
        def _():
            for copy in copies1(nwin - 1, False) + copies1(0, True):
                copy.wait()

        @pl.when(i == 1)
        def _():
            for copy in copies1(0, False):
                copy.wait()

        @pl.when((i > 0) & (i < nwin - 1))
        def _():
            for copy in copies1(i, False):
                copy.wait()

        state = jnp.where(zlow == 1, natural1(w + 1), natural1(w))
        key_mask, query_mask = labels(w)
        out = block(state, key_mask, query_mask, *weights(1))
        put(r2, w + 1, out)
        for copy in copies2(w, False):
            copy.start()

        @pl.when(w == nwin - 1)
        def _():
            for copy in copies2(nwin - 1, True):
                copy.start()

        return carry

    lax.fori_loop(0, nwin, second, 0)

    loads[8].wait()
    for dy in range(3):
        for dz in range(3):
            cw[dy, dz * width : (dz + 1) * width, :] = jnp.concatenate(
                [cw_ref[9 * dx + 3 * dy + dz].astype(F32) for dx in range(3)], 1
            ).astype(BF16)

    py = sy + 2

    def spread(jj, partial):
        low_at = lax.rem(jj + nwin, nwin + 1)
        high_at = jnp.where(partial, low_at, lax.rem(jj, nwin + 1))
        outer = jnp.where((jj == 0) | (jj == nwin + 1), 1, 0)
        above = jnp.where(here[2] < count[2] - 1, 1, 0)
        below = jnp.where(here[2] > 0, 1, 0)
        keep = jnp.where(zlow == 1, jnp.maximum(above, 1 - outer), jnp.maximum(below, 1 - outer))
        for source in range(4):
            tiles = []
            for tile in range(TILES):
                part = slice(tile * LANE, (tile + 1) * LANE)
                value = jnp.where(
                    zlow[:, part] == 1,
                    r2[source, low_at, tile].astype(F32),
                    r2[source, high_at, tile].astype(F32),
                )
                tiles.append(jnp.where(keep[:, part] == 1, value, 0.0))
            rows_s[source] = jnp.concatenate(tiles, 1).T
        for x in range(-1, sx + 1):
            for y in range(-1, sy + 1):
                ok = None
                fromx = x < SHIFT
                fromy = y < SHIFT
                for at, axis, size in ((x, 0, sx), (y, 1, sy)):
                    if at == -1:
                        test = here[axis] > 0
                    elif at == size:
                        test = here[axis] < count[axis] - 1
                    else:
                        continue
                    ok = test if ok is None else ok & test
                source = int(fromx) + 2 * int(fromy)
                lane = PLACE[x % WINDOW, y % WINDOW]
                value = rows_s[source, pl.ds(lane, WINDOW), :]
                if ok is not None:
                    value = jnp.where(ok, value, 0.0)
                pad[(x + 1) * py + y + 1, pl.ds(1 + WINDOW * jj, WINDOW), :] = value

    deep = cols.shape[1]

    def convolve(chunk):
        base = WINDOW + chunk * deep

        def stack(xp, carry):
            for y in range(py):
                at = xp * py + y
                cols[at] = jnp.concatenate(
                    [pad[at, base + dz : base + dz + deep, :] for dz in range(3)], 1
                ).astype(BF16)
            total = None
            for dy in range(3):
                piece = cols[pl.ds(xp * py + dy, sy)].reshape(sy * deep, 3 * width)
                part = dot(piece, cw[dy])
                total = part if total is None else total + part
            ys[xp] = total
            return carry

        lax.fori_loop(0, sx + 2, stack, 0)
        size = min(deep, sz - chunk * deep)

        def finish(x, carry):
            total = (
                ys[x][:, :width]
                + ys[x + 1][:, width : 2 * width]
                + ys[x + 2][:, 2 * width : 3 * width]
            )
            value = norm_rows(total, cg_ref[...])
            value = jnp.where(value >= 0, value, 0.01 * value).reshape(sy, deep, width)
            centre = pad[pl.ds((x + 1) * py + 1, sy), base + 1 : base + 1 + deep, :]
            out_ref[x, :, chunk * deep : chunk * deep + size, :] = (centre + value)[
                :, :size
            ].astype(BF16)
            return carry

        lax.fori_loop(0, sx, finish, 0)

    for w in range(nwin):
        if w != nwin - 2:
            for copy in copies2(w, False):
                copy.wait()
    for copy in copies2(nwin - 1, True):
        copy.wait()

    def spread_early(i, carry):
        spread(lax.rem(i + nwin + 1, nwin + 2), i == nwin)
        return carry

    def spread_late(i, carry):
        spread(i, False)
        return carry

    lax.fori_loop(0, nwin + 1, spread_early, 0)
    chunks = -(-sz // deep)
    early = sum(deep * (c + 1) < WINDOW * (nwin - 2) + SHIFT for c in range(chunks))
    for c in range(early):
        convolve(c)
    for copy in copies2(nwin - 2, False):
        copy.wait()
    lax.fori_loop(nwin - 1, nwin + 1, spread_late, 0)
    for c in range(early, chunks):
        convolve(c)


def body(volume, w_qkv, w_proj, w_up, w_down, norm_gain, conv_weight, conv_gain):
    sx, sy, sz, width = volume.shape
    assert sx == WINDOW and sy == WINDOW and sz % WINDOW == 0
    nwin = sz // WINDOW
    hidden = w_up.shape[-1]
    deep = -(-sz // 16) * 16
    tall = -(-(WINDOW + 2 + max(deep, sz + WINDOW)) // 8) * 8
    ncopy = 3 * nwin + 4
    padded = (sx + 2) * (sy + 2)
    vmem = pl.BlockSpec(memory_space=pltpu.VMEM)
    sems = [pltpu.SemaphoreType.DMA((ncopy,))] * 4
    operands = (
        jnp.asarray(lane_facts()), volume, w_qkv, w_proj, w_up, jnp.swapaxes(w_down, 1, 2),
        norm_gain, conv_weight, conv_gain.reshape(1, width),
    )
    return pl.pallas_call(
        functools.partial(kernel, (sx, sy, sz, width)),
        out_shape=jax.ShapeDtypeStruct(volume.shape, BF16),
        in_specs=[pl.BlockSpec(memory_space=pltpu.HBM)] * 9,
        out_specs=vmem,
        scratch_shapes=[pltpu.VMEM(o.shape, o.dtype) for o in operands]
        + [
            pltpu.VMEM((sx * sy, deep, width), F32),
            pltpu.VMEM((nwin, LANES, width), F32),
            pltpu.VMEM((4, nwin + 1, TILES, width, LANE), BF16),
            pltpu.VMEM((4, nwin + 1, TILES, width, LANE), BF16),
            pltpu.VMEM((2, 3 * width, width), BF16),
            pltpu.VMEM((2, width, width), BF16),
            pltpu.VMEM((2, hidden, width), BF16),
            pltpu.VMEM((2, 2, width, LANES), F32),
            pltpu.VMEM((4, LANES, width), F32),
            pltpu.VMEM((padded, tall, width), F32),
            pltpu.VMEM((padded, 16, 3 * width), BF16),
            pltpu.VMEM((3, 3 * width, 3 * width), BF16),
            pltpu.VMEM((sx + 2, sy * 16, 3 * width), F32),
        ]
        + sems
        + [pltpu.SemaphoreType.DMA((9,))],
        compiler_params=pltpu.CompilerParams(
            collective_id=0, has_side_effects=True, vmem_limit_bytes=64 * 1024 * 1024 - 65536
        ),
    )(*operands)


def solution(mesh):
    placed = (P(("parts", "gx"), "gy", "gz", None), P(), P(), P(), P(), P(), P(), P())
    return jax.shard_map(
        body,
        mesh=mesh,
        in_specs=placed,
        out_specs=P(("parts", "gx"), "gy", "gz", None),
        check_vma=False,
    )
```

```python
import functools
import itertools

import jax
import jax.numpy as jnp
import numpy as np
from jax import lax
from jax.experimental import pallas as pl
from jax.experimental.pallas import tpu as pltpu
from jax.sharding import PartitionSpec as P

HEADS = 3
WINDOW = 7
SHIFT = 3
LANE = 128
TILES = 3
LANES = TILES * LANE
MESH = pl.DeviceIdType.MESH
F32 = jnp.float32
BF16 = jnp.bfloat16


def column_lanes():
    low, high = range(SHIFT), range(SHIFT, WINDOW)
    both = list(itertools.product(low, low))
    first = list(itertools.product(low, high)) + both[:6]
    second = list(itertools.product(high, low)) + both[6:]
    groups = (list(itertools.product(high, high)), first, second)
    place = {}
    for tile, group in enumerate(groups):
        for at, column in enumerate(group):
            place[column] = tile * LANE + at * WINDOW
    return place


PLACE = column_lanes()


def lane_facts():
    facts = np.zeros((8, LANES), np.int32)
    for (x, y), lane in PLACE.items():
        for z in range(WINDOW):
            facts[0, lane + z] = x < SHIFT
            facts[1, lane + z] = y < SHIFT
            facts[2, lane + z] = z < SHIFT
            facts[3, lane + z] = 1
    return facts


def norm_columns(values, gain):
    mean = jnp.mean(values, 0, keepdims=True)
    centred = values - mean
    spread = jnp.mean(centred * centred, 0, keepdims=True)
    return centred * lax.rsqrt(spread + 1e-05) * gain


def norm_rows(values, gain):
    mean = jnp.mean(values, -1, keepdims=True)
    centred = values - mean
    spread = jnp.mean(centred * centred, -1, keepdims=True)
    return centred * lax.rsqrt(spread + 1e-05) * gain


def dot(a, b):
    return jnp.dot(a, b, preferred_element_type=F32)


def block(state, key_mask, query_mask, w_qkv, w_proj, w_up, w_down, gain0, gain1):
    width = state.shape[0]
    depth = width // HEADS
    normed = norm_columns(state, gain0).astype(BF16)
    qkv = dot(w_qkv, normed)
    scale = depth ** (-0.5) * np.log2(np.e)
    query = (qkv[:width] * scale).astype(BF16)
    keys = qkv[width : 2 * width].astype(BF16)
    vals = qkv[2 * width :].astype(BF16)
    ones = jnp.ones((16, LANES), BF16)
    mixed = []
    for head in range(HEADS):
        rows = slice(head * depth, (head + 1) * depth)
        q = jnp.concatenate([query[rows], query_mask], 0)
        k = jnp.concatenate([keys[rows], key_mask], 0)
        scores = lax.dot_general(k, q, (((0,), (0,)), ((), ())), preferred_element_type=F32)
        top = jnp.max(scores, 0, keepdims=True)
        weights = jnp.exp2(scores - top).astype(BF16)
        both = dot(jnp.concatenate([vals[rows], ones], 0), weights)
        mixed.append(both[:depth] / both[depth : depth + 1])
    mixed = jnp.concatenate(mixed, 0).astype(BF16)
    state = (state + dot(w_proj, mixed)).astype(BF16).astype(F32)
    normed = norm_columns(state, gain1).astype(BF16)
    upper = jax.nn.gelu(dot(w_up, normed)).astype(BF16)
    return (state + dot(w_down, upper)).astype(BF16)


def kernel(
    sizes, facts_in, vol_in, wqkv_in, wproj_in, wup_in, tdown_in, gain_in, cw_in, cg_in,
    out_ref, facts_ref, vol_ref, wqkv_ref, wproj_ref, wup_ref, tdown, gain_ref, cw_ref, cg_ref,
    wide, win, r1, r2, tqkv, tproj, tup, tgain, rows_s, pad, cols, cw, ys,
    send1, recv1, send2, recv2, loaded,
):
    pairs = (
        (vol_in, vol_ref), (wqkv_in, wqkv_ref), (wproj_in, wproj_ref), (wup_in, wup_ref),
        (gain_in, gain_ref), (tdown_in, tdown), (facts_in, facts_ref), (cg_in, cg_ref),
        (cw_in, cw_ref),
    )
    loads = [pltpu.make_async_copy(a, b, loaded.at[i]) for i, (a, b) in enumerate(pairs)]
    for load in loads:
        load.start()

    sx, sy, sz, width = sizes
    nwin = sz // WINDOW
    axes = ("gx", "gy", "gz")
    here = [lax.axis_index(a) for a in axes]
    count = [lax.axis_size(a) for a in axes]

    def device(steps, sign):
        return {
            a: lax.rem(here[i] + sign * steps[i] + count[i], count[i]) for i, a in enumerate(axes)
        }

    others = [s for s in itertools.product((0, 1), repeat=3) if any(s)]
    barrier = pltpu.get_barrier_semaphore()
    for steps in others:
        for sign in (-1, 1):
            pl.semaphore_signal(barrier, inc=1, device_id=device(steps, sign), device_id_type=MESH)

    for load in loads[1:8]:
        load.wait()
    for b in range(2):
        tqkv[b] = wqkv_ref[b].astype(F32).T.astype(BF16)
        tproj[b] = wproj_ref[b].astype(F32).T.astype(BF16)
        tup[b] = wup_ref[b].astype(F32).T.astype(BF16)
        for i in range(2):
            wide_gain = jnp.broadcast_to(gain_ref[b, i : i + 1, :], (LANE, width)).T
            tgain[b, i] = jnp.concatenate([wide_gain] * TILES, 1)
    win[...] = jnp.zeros_like(win)
    loads[0].wait()
    wide[:, :sz, :] = vol_ref[...].reshape(sx * sy, sz, width).astype(F32)

    def gather(w, carry):
        for (x, y), lane in PLACE.items():
            win[w, pl.ds(lane, WINDOW), :] = wide[x * sy + y, pl.ds(w * WINDOW, WINDOW), :]
        return carry

    lax.fori_loop(0, nwin, gather, 0)

    xlow, ylow, zlow, valid = [facts_ref[i : i + 1, :] for i in range(4)]
    last = [jnp.where(here[i] == count[i] - 1, 1, 0) for i in range(3)]
    row = lax.broadcasted_iota(jnp.int32, (16, LANES), 0)

    def masks(code):
        key = jnp.where(row == 8, 1 - valid, jnp.where(row == code, valid, 0))
        query = jnp.where(row == code, 0.0, jnp.where(row <= 8, -1e30, 0.0))
        return key.astype(F32).astype(BF16), query.astype(BF16)

    def labels(w):
        edge = last[2] * jnp.where(w == nwin - 1, 1, 0)
        return masks(4 * last[0] * xlow + 2 * last[1] * ylow + edge * zlow)

    def weights(b):
        return tqkv[b], tproj[b], tup[b], tdown[b], tgain[b, 0], tgain[b, 1]

    def put(ref, at, value):
        for tile in range(TILES):
            ref[0, at, tile] = value[:, tile * LANE : (tile + 1) * LANE]

    spans = {0: (0, 1), 1: (1, 1), 2: (2, 1), 3: (1, 2)}

    def copies1(w, across):
        found = []
        for source in range(0 if across else 1, 4):
            start, size = spans[source]
            steps = (source % 2, source // 2, 1 if across else 0)
            sem = 3 * nwin + source if across else 3 * w + source - 1
            found.append(
                pltpu.make_async_remote_copy(
                    src_ref=r1.at[0, w, pl.ds(start, size)],
                    dst_ref=r1.at[source, nwin if across else w, pl.ds(start, size)],
                    send_sem=send1.at[sem],
                    recv_sem=recv1.at[sem],
                    device_id=device(steps, -1),
                    device_id_type=MESH,
                )
            )
        return found

    def copies2(w, across):
        found = []
        for source in range(0 if across else 1, 4):
            steps = (source % 2, source // 2, 1 if across else 0)
            sem = 3 * nwin + source if across else 3 * w + source - 1
            found.append(
                pltpu.make_async_remote_copy(
                    src_ref=r2.at[0, w + 1],
                    dst_ref=r2.at[source, 0 if across else w + 1],
                    send_sem=send2.at[sem],
                    recv_sem=recv2.at[sem],
                    device_id=device(steps, 1),
                    device_id_type=MESH,
                )
            )
        return found

    plain_key, plain_query = masks(jnp.zeros((1, LANES), jnp.int32))

    def first(i, carry):
        pair = [lax.rem(2 * i + at + nwin - 1, nwin) for at in range(2)]
        outs = [block(win[w].T, plain_key, plain_query, *weights(0)) for w in pair]
        for w, out in zip(pair, outs):
            put(r1, w, out)

        @pl.when(i == 0)
        def _():
            pl.semaphore_wait(barrier, 2 * len(others))

        for w in pair:
            for copy in copies1(w, False):
                copy.start()

        @pl.when(i == 0)
        def _():
            for copy in copies1(0, True):
                copy.start()

        return carry

    lax.fori_loop(0, nwin // 2, first, 0)

    def natural1(j):
        both = (xlow * ylow) == 1
        one = both[:, LANE : 2 * LANE]
        two = both[:, 2 * LANE :]
        return jnp.concatenate(
            [
                r1[0, j, 0].astype(F32),
                jnp.where(one, r1[3, j, 1].astype(F32), r1[1, j, 1].astype(F32)),
                jnp.where(two, r1[3, j, 2].astype(F32), r1[2, j, 2].astype(F32)),
            ],
            1,
        )

    def second(i, carry):
        w = lax.rem(i + nwin - 1, nwin)

        @pl.when(i == 0)
        def _():
            for copy in copies1(nwin - 1, False) + copies1(0, True):
                copy.wait()

        @pl.when(i == 1)
        def _():
            for copy in copies1(0, False):
                copy.wait()

        @pl.when((i > 0) & (i < nwin - 1))
        def _():
            for copy in copies1(i, False):
                copy.wait()

        state = jnp.where(zlow == 1, natural1(w + 1), natural1(w))
        key_mask, query_mask = labels(w)
        out = block(state, key_mask, query_mask, *weights(1))
        put(r2, w + 1, out)
        for copy in copies2(w, False):
            copy.start()

        @pl.when(w == nwin - 1)
        def _():
            for copy in copies2(nwin - 1, True):
                copy.start()

        return carry

    lax.fori_loop(0, nwin, second, 0)

    loads[8].wait()
    for dy in range(3):
        for dz in range(3):
            cw[dy, dz * width : (dz + 1) * width, :] = jnp.concatenate(
                [cw_ref[9 * dx + 3 * dy + dz].astype(F32) for dx in range(3)], 1
            ).astype(BF16)

    py = sy + 2

    def spread(jj, partial):
        low_at = lax.rem(jj + nwin, nwin + 1)
        high_at = jnp.where(partial, low_at, lax.rem(jj, nwin + 1))
        outer = jnp.where((jj == 0) | (jj == nwin + 1), 1, 0)
        above = jnp.where(here[2] < count[2] - 1, 1, 0)
        below = jnp.where(here[2] > 0, 1, 0)
        keep = jnp.where(zlow == 1, jnp.maximum(above, 1 - outer), jnp.maximum(below, 1 - outer))
        for source in range(4):
            tiles = []
            for tile in range(TILES):
                part = slice(tile * LANE, (tile + 1) * LANE)
                value = jnp.where(
                    zlow[:, part] == 1,
                    r2[source, low_at, tile].astype(F32),
                    r2[source, high_at, tile].astype(F32),
                )
                tiles.append(jnp.where(keep[:, part] == 1, value, 0.0))
            rows_s[source] = jnp.concatenate(tiles, 1).T
        for x in range(-1, sx + 1):
            for y in range(-1, sy + 1):
                ok = None
                fromx = x < SHIFT
                fromy = y < SHIFT
                for at, axis, size in ((x, 0, sx), (y, 1, sy)):
                    if at == -1:
                        test = here[axis] > 0
                    elif at == size:
                        test = here[axis] < count[axis] - 1
                    else:
                        continue
                    ok = test if ok is None else ok & test
                source = int(fromx) + 2 * int(fromy)
                lane = PLACE[x % WINDOW, y % WINDOW]
                value = rows_s[source, pl.ds(lane, WINDOW), :]
                if ok is not None:
                    value = jnp.where(ok, value, 0.0)
                pad[(x + 1) * py + y + 1, pl.ds(1 + WINDOW * jj, WINDOW), :] = value

    deep = cols.shape[1]

    def convolve(chunk):
        base = WINDOW + chunk * deep

        def stack(xp, carry):
            for y in range(py):
                at = xp * py + y
                cols[at] = jnp.concatenate(
                    [pad[at, base + dz : base + dz + deep, :] for dz in range(3)], 1
                ).astype(BF16)
            total = None
            for dy in range(3):
                piece = cols[pl.ds(xp * py + dy, sy)].reshape(sy * deep, 3 * width)
                part = dot(piece, cw[dy])
                total = part if total is None else total + part
            ys[xp] = total
            return carry

        lax.fori_loop(0, sx + 2, stack, 0)
        size = min(deep, sz - chunk * deep)

        def finish(x, carry):
            total = (
                ys[x][:, :width]
                + ys[x + 1][:, width : 2 * width]
                + ys[x + 2][:, 2 * width : 3 * width]
            )
            value = norm_rows(total, cg_ref[...])
            value = jnp.where(value >= 0, value, 0.01 * value).reshape(sy, deep, width)
            centre = pad[pl.ds((x + 1) * py + 1, sy), base + 1 : base + 1 + deep, :]
            out_ref[x, :, chunk * deep : chunk * deep + size, :] = (centre + value)[
                :, :size
            ].astype(BF16)
            return carry

        lax.fori_loop(0, sx, finish, 0)

    for w in range(nwin):
        if w != nwin - 2:
            for copy in copies2(w, False):
                copy.wait()
    for copy in copies2(nwin - 1, True):
        copy.wait()

    def spread_early(i, carry):
        spread(lax.rem(i + nwin + 1, nwin + 2), i == nwin)
        return carry

    def spread_late(i, carry):
        spread(i, False)
        return carry

    lax.fori_loop(0, nwin + 1, spread_early, 0)
    chunks = -(-sz // deep)
    early = sum(deep * (c + 1) < WINDOW * (nwin - 2) + SHIFT for c in range(chunks))
    for c in range(early):
        convolve(c)
    for copy in copies2(nwin - 2, False):
        copy.wait()
    lax.fori_loop(nwin - 1, nwin + 1, spread_late, 0)
    for c in range(early, chunks):
        convolve(c)


def body(volume, w_qkv, w_proj, w_up, w_down, norm_gain, conv_weight, conv_gain):
    sx, sy, sz, width = volume.shape
    assert sx == WINDOW and sy == WINDOW and sz % (2 * WINDOW) == 0
    nwin = sz // WINDOW
    hidden = w_up.shape[-1]
    deep = -(-sz // 16) * 16
    tall = -(-(WINDOW + 2 + max(deep, sz + WINDOW)) // 8) * 8
    ncopy = 3 * nwin + 4
    padded = (sx + 2) * (sy + 2)
    vmem = pl.BlockSpec(memory_space=pltpu.VMEM)
    sems = [pltpu.SemaphoreType.DMA((ncopy,))] * 4
    operands = (
        jnp.asarray(lane_facts()), volume, w_qkv, w_proj, w_up, jnp.swapaxes(w_down, 1, 2),
        norm_gain, conv_weight, conv_gain.reshape(1, width),
    )
    return pl.pallas_call(
        functools.partial(kernel, (sx, sy, sz, width)),
        out_shape=jax.ShapeDtypeStruct(volume.shape, BF16),
        in_specs=[pl.BlockSpec(memory_space=pltpu.HBM)] * 9,
        out_specs=vmem,
        scratch_shapes=[pltpu.VMEM(o.shape, o.dtype) for o in operands]
        + [
            pltpu.VMEM((sx * sy, deep, width), F32),
            pltpu.VMEM((nwin, LANES, width), F32),
            pltpu.VMEM((4, nwin + 1, TILES, width, LANE), BF16),
            pltpu.VMEM((4, nwin + 1, TILES, width, LANE), BF16),
            pltpu.VMEM((2, 3 * width, width), BF16),
            pltpu.VMEM((2, width, width), BF16),
            pltpu.VMEM((2, hidden, width), BF16),
            pltpu.VMEM((2, 2, width, LANES), F32),
            pltpu.VMEM((4, LANES, width), F32),
            pltpu.VMEM((padded, tall, width), F32),
            pltpu.VMEM((padded, 16, 3 * width), BF16),
            pltpu.VMEM((3, 3 * width, 3 * width), BF16),
            pltpu.VMEM((sx + 2, sy * 16, 3 * width), F32),
        ]
        + sems
        + [pltpu.SemaphoreType.DMA((9,))],
        compiler_params=pltpu.CompilerParams(
            collective_id=0, has_side_effects=True, vmem_limit_bytes=64 * 1024 * 1024 - 65536
        ),
    )(*operands)


def solution(mesh):
    placed = (P(("parts", "gx"), "gy", "gz", None), P(), P(), P(), P(), P(), P(), P())
    return jax.shard_map(
        body,
        mesh=mesh,
        in_specs=placed,
        out_specs=P(("parts", "gx"), "gy", "gz", None),
        check_vma=False,
    )
```

```python
import functools
import itertools

import jax
import jax.numpy as jnp
import numpy as np
from jax import lax
from jax.experimental import pallas as pl
from jax.experimental.pallas import tpu as pltpu
from jax.sharding import PartitionSpec as P

HEADS = 3
WINDOW = 7
SHIFT = 3
LANE = 128
TILES = 3
LANES = TILES * LANE
MESH = pl.DeviceIdType.MESH
F32 = jnp.float32
BF16 = jnp.bfloat16


def column_lanes():
    low, high = range(SHIFT), range(SHIFT, WINDOW)
    both = list(itertools.product(low, low))
    first = list(itertools.product(low, high)) + both[:6]
    second = list(itertools.product(high, low)) + both[6:]
    groups = (list(itertools.product(high, high)), first, second)
    place = {}
    for tile, group in enumerate(groups):
        for at, column in enumerate(group):
            place[column] = tile * LANE + at * WINDOW
    return place


PLACE = column_lanes()


def lane_facts():
    facts = np.zeros((8, LANES), np.int32)
    for (x, y), lane in PLACE.items():
        for z in range(WINDOW):
            facts[0, lane + z] = x < SHIFT
            facts[1, lane + z] = y < SHIFT
            facts[2, lane + z] = z < SHIFT
            facts[3, lane + z] = 1
    return facts


def norm_columns(values, gain):
    mean = jnp.mean(values, 0, keepdims=True)
    centred = values - mean
    spread = jnp.mean(centred * centred, 0, keepdims=True)
    return centred * lax.rsqrt(spread + 1e-05) * gain


def norm_rows(values, gain):
    mean = jnp.mean(values, -1, keepdims=True)
    centred = values - mean
    spread = jnp.mean(centred * centred, -1, keepdims=True)
    return centred * lax.rsqrt(spread + 1e-05) * gain


def dot(a, b):
    return jnp.dot(a, b, preferred_element_type=F32)


def block(state, key_mask, query_mask, w_qkv, w_proj, w_up, w_down, gain0, gain1):
    width = state.shape[0]
    depth = width // HEADS
    normed = norm_columns(state, gain0).astype(BF16)
    qkv = dot(w_qkv, normed)
    scale = depth ** (-0.5) * np.log2(np.e)
    query = (qkv[:width] * scale).astype(BF16)
    keys = qkv[width : 2 * width].astype(BF16)
    vals = qkv[2 * width :].astype(BF16)
    ones = jnp.ones((16, LANES), BF16)
    mixed = []
    for head in range(HEADS):
        rows = slice(head * depth, (head + 1) * depth)
        q = jnp.concatenate([query[rows], query_mask], 0)
        k = jnp.concatenate([keys[rows], key_mask], 0)
        scores = lax.dot_general(k, q, (((0,), (0,)), ((), ())), preferred_element_type=F32)
        top = jnp.max(scores, 0, keepdims=True)
        weights = jnp.exp2(scores - top).astype(BF16)
        both = dot(jnp.concatenate([vals[rows], ones], 0), weights)
        mixed.append(both[:depth] / both[depth : depth + 1])
    mixed = jnp.concatenate(mixed, 0).astype(BF16)
    state = (state + dot(w_proj, mixed)).astype(BF16).astype(F32)
    normed = norm_columns(state, gain1).astype(BF16)
    upper = jax.nn.gelu(dot(w_up, normed)).astype(BF16)
    return (state + dot(w_down, upper)).astype(BF16)


def kernel(
    sizes, facts_in, vol_in, wqkv_in, wproj_in, wup_in, tdown_in, gain_in, cw_in, cg_in,
    out_ref, facts_ref, vol_ref, wqkv_ref, wproj_ref, wup_ref, tdown, gain_ref, cw_ref, cg_ref,
    wide, win, r1, r2, tqkv, tproj, tup, tgain, rows_s, pad, cols, cw, ys,
    send1, recv1, send2, recv2, loaded,
):
    pairs = (
        (vol_in, vol_ref), (wqkv_in, wqkv_ref), (wproj_in, wproj_ref), (wup_in, wup_ref),
        (gain_in, gain_ref), (tdown_in, tdown), (facts_in, facts_ref), (cg_in, cg_ref),
        (cw_in, cw_ref),
    )
    loads = [pltpu.make_async_copy(a, b, loaded.at[i]) for i, (a, b) in enumerate(pairs)]
    for load in loads:
        load.start()

    sx, sy, sz, width = sizes
    nwin = sz // WINDOW
    axes = ("gx", "gy", "gz")
    here = [lax.axis_index(a) for a in axes]
    count = [lax.axis_size(a) for a in axes]

    def device(steps, sign):
        return {
            a: lax.rem(here[i] + sign * steps[i] + count[i], count[i]) for i, a in enumerate(axes)
        }

    others = [s for s in itertools.product((0, 1), repeat=3) if any(s)]
    barrier = pltpu.get_barrier_semaphore()
    for steps in others:
        for sign in (-1, 1):
            pl.semaphore_signal(barrier, inc=1, device_id=device(steps, sign), device_id_type=MESH)

    for load in loads[1:8]:
        load.wait()
    for b in range(2):
        tqkv[b] = wqkv_ref[b].astype(F32).T.astype(BF16)
        tproj[b] = wproj_ref[b].astype(F32).T.astype(BF16)
        tup[b] = wup_ref[b].astype(F32).T.astype(BF16)
        for i in range(2):
            wide_gain = jnp.broadcast_to(gain_ref[b, i : i + 1, :], (LANE, width)).T
            tgain[b, i] = jnp.concatenate([wide_gain] * TILES, 1)
    win[...] = jnp.zeros_like(win)
    loads[0].wait()
    wide[:, :sz, :] = vol_ref[...].reshape(sx * sy, sz, width).astype(F32)

    def gather(w, carry):
        for (x, y), lane in PLACE.items():
            win[w, pl.ds(lane, WINDOW), :] = wide[x * sy + y, pl.ds(w * WINDOW, WINDOW), :]
        return carry

    lax.fori_loop(0, nwin, gather, 0)

    xlow, ylow, zlow, valid = [facts_ref[i : i + 1, :] for i in range(4)]
    last = [jnp.where(here[i] == count[i] - 1, 1, 0) for i in range(3)]
    row = lax.broadcasted_iota(jnp.int32, (16, LANES), 0)

    def masks(code):
        key = jnp.where(row == 8, 1 - valid, jnp.where(row == code, valid, 0))
        query = jnp.where(row == code, 0.0, jnp.where(row <= 8, -1e30, 0.0))
        return key.astype(F32).astype(BF16), query.astype(BF16)

    def labels(w):
        edge = last[2] * jnp.where(w == nwin - 1, 1, 0)
        return masks(4 * last[0] * xlow + 2 * last[1] * ylow + edge * zlow)

    def weights(b):
        return tqkv[b], tproj[b], tup[b], tdown[b], tgain[b, 0], tgain[b, 1]

    def put(ref, at, value):
        for tile in range(TILES):
            ref[0, at, tile] = value[:, tile * LANE : (tile + 1) * LANE]

    spans = {0: (0, 1), 1: (1, 1), 2: (2, 1), 3: (1, 2)}

    def copies1(w, across):
        found = []
        for source in range(0 if across else 1, 4):
            start, size = spans[source]
            steps = (source % 2, source // 2, 1 if across else 0)
            sem = 3 * nwin + source if across else 3 * w + source - 1
            found.append(
                pltpu.make_async_remote_copy(
                    src_ref=r1.at[0, w, pl.ds(start, size)],
                    dst_ref=r1.at[source, nwin if across else w, pl.ds(start, size)],
                    send_sem=send1.at[sem],
                    recv_sem=recv1.at[sem],
                    device_id=device(steps, -1),
                    device_id_type=MESH,
                )
            )
        return found

    def copies2(w, across):
        found = []
        for source in range(0 if across else 1, 4):
            steps = (source % 2, source // 2, 1 if across else 0)
            sem = 3 * nwin + source if across else 3 * w + source - 1
            found.append(
                pltpu.make_async_remote_copy(
                    src_ref=r2.at[0, w + 1],
                    dst_ref=r2.at[source, 0 if across else w + 1],
                    send_sem=send2.at[sem],
                    recv_sem=recv2.at[sem],
                    device_id=device(steps, 1),
                    device_id_type=MESH,
                )
            )
        return found

    plain_key, plain_query = masks(jnp.zeros((1, LANES), jnp.int32))

    def first(i, carry):
        pair = [lax.rem(2 * i + at + nwin - 1, nwin) for at in range(2)]
        outs = [block(win[w].T, plain_key, plain_query, *weights(0)) for w in pair]
        for w, out in zip(pair, outs):
            put(r1, w, out)

        @pl.when(i == 0)
        def _():
            pl.semaphore_wait(barrier, 2 * len(others))

        for w in pair:
            for copy in copies1(w, False):
                copy.start()

        @pl.when(i == 0)
        def _():
            for copy in copies1(0, True):
                copy.start()

        return carry

    lax.fori_loop(0, nwin // 2, first, 0)

    def natural1(j):
        both = (xlow * ylow) == 1
        one = both[:, LANE : 2 * LANE]
        two = both[:, 2 * LANE :]
        return jnp.concatenate(
            [
                r1[0, j, 0].astype(F32),
                jnp.where(one, r1[3, j, 1].astype(F32), r1[1, j, 1].astype(F32)),
                jnp.where(two, r1[3, j, 2].astype(F32), r1[2, j, 2].astype(F32)),
            ],
            1,
        )

    def second(i, carry):
        w = lax.rem(i + nwin - 1, nwin)

        @pl.when(i == 0)
        def _():
            for copy in copies1(nwin - 1, False) + copies1(0, True):
                copy.wait()

        @pl.when(i == 1)
        def _():
            for copy in copies1(0, False):
                copy.wait()

        @pl.when((i > 0) & (i < nwin - 1))
        def _():
            for copy in copies1(i, False):
                copy.wait()

        state = jnp.where(zlow == 1, natural1(w + 1), natural1(w))
        key_mask, query_mask = labels(w)
        out = block(state, key_mask, query_mask, *weights(1))
        put(r2, w + 1, out)
        for copy in copies2(w, False):
            copy.start()

        @pl.when(w == nwin - 1)
        def _():
            for copy in copies2(nwin - 1, True):
                copy.start()

        return carry

    lax.fori_loop(0, nwin, second, 0)

    loads[8].wait()
    for dy in range(3):
        for dz in range(3):
            cw[dy, dz * width : (dz + 1) * width, :] = jnp.concatenate(
                [cw_ref[9 * dx + 3 * dy + dz].astype(F32) for dx in range(3)], 1
            ).astype(BF16)

    py = sy + 2

    def spread(jj, partial):
        low_at = lax.rem(jj + nwin, nwin + 1)
        high_at = jnp.where(partial, low_at, lax.rem(jj, nwin + 1))
        outer = jnp.where((jj == 0) | (jj == nwin + 1), 1, 0)
        above = jnp.where(here[2] < count[2] - 1, 1, 0)
        below = jnp.where(here[2] > 0, 1, 0)
        keep = jnp.where(zlow == 1, jnp.maximum(above, 1 - outer), jnp.maximum(below, 1 - outer))
        for source in range(4):
            tiles = []
            for tile in range(TILES):
                part = slice(tile * LANE, (tile + 1) * LANE)
                value = jnp.where(
                    zlow[:, part] == 1,
                    r2[source, low_at, tile].astype(F32),
                    r2[source, high_at, tile].astype(F32),
                )
                tiles.append(jnp.where(keep[:, part] == 1, value, 0.0))
            rows_s[source] = jnp.concatenate(tiles, 1).T
        for x in range(-1, sx + 1):
            for y in range(-1, sy + 1):
                ok = None
                fromx = x < SHIFT
                fromy = y < SHIFT
                for at, axis, size in ((x, 0, sx), (y, 1, sy)):
                    if at == -1:
                        test = here[axis] > 0
                    elif at == size:
                        test = here[axis] < count[axis] - 1
                    else:
                        continue
                    ok = test if ok is None else ok & test
                source = int(fromx) + 2 * int(fromy)
                lane = PLACE[x % WINDOW, y % WINDOW]
                value = rows_s[source, pl.ds(lane, WINDOW), :]
                if ok is not None:
                    value = jnp.where(ok, value, 0.0)
                pad[(x + 1) * py + y + 1, pl.ds(1 + WINDOW * jj, WINDOW), :] = value

    deep = cols.shape[1]

    def convolve(chunk):
        base = WINDOW + chunk * deep

        def stack(xp, carry):
            for y in range(py):
                at = xp * py + y
                cols[at] = jnp.concatenate(
                    [pad[at, base + dz : base + dz + deep, :] for dz in range(3)], 1
                ).astype(BF16)
            total = None
            for dy in range(3):
                piece = cols[pl.ds(xp * py + dy, sy)].reshape(sy * deep, 3 * width)
                part = dot(piece, cw[dy])
                total = part if total is None else total + part
            ys[xp] = total
            return carry

        lax.fori_loop(0, sx + 2, stack, 0, unroll=3)
        size = min(deep, sz - chunk * deep)

        def finish(x, carry):
            total = (
                ys[x][:, :width]
                + ys[x + 1][:, width : 2 * width]
                + ys[x + 2][:, 2 * width : 3 * width]
            )
            value = norm_rows(total, cg_ref[...])
            value = jnp.where(value >= 0, value, 0.01 * value).reshape(sy, deep, width)
            centre = pad[pl.ds((x + 1) * py + 1, sy), base + 1 : base + 1 + deep, :]
            out_ref[x, :, chunk * deep : chunk * deep + size, :] = (centre + value)[
                :, :size
            ].astype(BF16)
            return carry

        lax.fori_loop(0, sx, finish, 0, unroll=True)

    for w in range(nwin):
        if w != nwin - 2:
            for copy in copies2(w, False):
                copy.wait()
    for copy in copies2(nwin - 1, True):
        copy.wait()

    def spread_early(i, carry):
        spread(lax.rem(i + nwin + 1, nwin + 2), i == nwin)
        return carry

    def spread_late(i, carry):
        spread(i, False)
        return carry

    lax.fori_loop(0, nwin + 1, spread_early, 0)
    chunks = -(-sz // deep)
    early = sum(deep * (c + 1) < WINDOW * (nwin - 2) + SHIFT for c in range(chunks))
    for c in range(early):
        convolve(c)
    for copy in copies2(nwin - 2, False):
        copy.wait()
    lax.fori_loop(nwin - 1, nwin + 1, spread_late, 0)
    for c in range(early, chunks):
        convolve(c)


def body(volume, w_qkv, w_proj, w_up, w_down, norm_gain, conv_weight, conv_gain):
    sx, sy, sz, width = volume.shape
    assert sx == WINDOW and sy == WINDOW and sz % (2 * WINDOW) == 0
    nwin = sz // WINDOW
    hidden = w_up.shape[-1]
    deep = -(-sz // 16) * 16
    tall = -(-(WINDOW + 2 + max(deep, sz + WINDOW)) // 8) * 8
    ncopy = 3 * nwin + 4
    padded = (sx + 2) * (sy + 2)
    vmem = pl.BlockSpec(memory_space=pltpu.VMEM)
    sems = [pltpu.SemaphoreType.DMA((ncopy,))] * 4
    operands = (
        jnp.asarray(lane_facts()), volume, w_qkv, w_proj, w_up, jnp.swapaxes(w_down, 1, 2),
        norm_gain, conv_weight, conv_gain.reshape(1, width),
    )
    return pl.pallas_call(
        functools.partial(kernel, (sx, sy, sz, width)),
        out_shape=jax.ShapeDtypeStruct(volume.shape, BF16),
        in_specs=[pl.BlockSpec(memory_space=pltpu.HBM)] * 9,
        out_specs=vmem,
        scratch_shapes=[pltpu.VMEM(o.shape, o.dtype) for o in operands]
        + [
            pltpu.VMEM((sx * sy, deep, width), F32),
            pltpu.VMEM((nwin, LANES, width), F32),
            pltpu.VMEM((4, nwin + 1, TILES, width, LANE), BF16),
            pltpu.VMEM((4, nwin + 1, TILES, width, LANE), BF16),
            pltpu.VMEM((2, 3 * width, width), BF16),
            pltpu.VMEM((2, width, width), BF16),
            pltpu.VMEM((2, hidden, width), BF16),
            pltpu.VMEM((2, 2, width, LANES), F32),
            pltpu.VMEM((4, LANES, width), F32),
            pltpu.VMEM((padded, tall, width), F32),
            pltpu.VMEM((padded, 16, 3 * width), BF16),
            pltpu.VMEM((3, 3 * width, 3 * width), BF16),
            pltpu.VMEM((sx + 2, sy * 16, 3 * width), F32),
        ]
        + sems
        + [pltpu.SemaphoreType.DMA((9,))],
        compiler_params=pltpu.CompilerParams(
            collective_id=0, has_side_effects=True, vmem_limit_bytes=64 * 1024 * 1024 - 65536
        ),
    )(*operands)


def solution(mesh):
    placed = (P(("parts", "gx"), "gy", "gz", None), P(), P(), P(), P(), P(), P(), P())
    return jax.shard_map(
        body,
        mesh=mesh,
        in_specs=placed,
        out_specs=P(("parts", "gx"), "gy", "gz", None),
        check_vma=False,
    )
```

```python
import functools
import itertools

import jax
import jax.numpy as jnp
import numpy as np
from jax import lax
from jax.experimental import pallas as pl
from jax.experimental.pallas import tpu as pltpu
from jax.sharding import PartitionSpec as P

HEADS = 3
WINDOW = 7
SHIFT = 3
LANE = 128
TILES = 3
LANES = TILES * LANE
MESH = pl.DeviceIdType.MESH
F32 = jnp.float32
BF16 = jnp.bfloat16


def column_lanes():
    low, high = range(SHIFT), range(SHIFT, WINDOW)
    both = list(itertools.product(low, low))
    first = list(itertools.product(low, high)) + both[:6]
    second = list(itertools.product(high, low)) + both[6:]
    groups = (list(itertools.product(high, high)), first, second)
    place = {}
    for tile, group in enumerate(groups):
        for at, column in enumerate(group):
            place[column] = tile * LANE + at * WINDOW
    return place


PLACE = column_lanes()


def lane_facts():
    facts = np.zeros((8, LANES), np.int32)
    for (x, y), lane in PLACE.items():
        for z in range(WINDOW):
            facts[0, lane + z] = x < SHIFT
            facts[1, lane + z] = y < SHIFT
            facts[2, lane + z] = z < SHIFT
            facts[3, lane + z] = 1
    return facts


def norm_columns(values, gain):
    mean = jnp.mean(values, 0, keepdims=True)
    centred = values - mean
    spread = jnp.mean(centred * centred, 0, keepdims=True)
    return centred * lax.rsqrt(spread + 1e-05) * gain


def norm_rows(values, gain):
    mean = jnp.mean(values, -1, keepdims=True)
    centred = values - mean
    spread = jnp.mean(centred * centred, -1, keepdims=True)
    return centred * lax.rsqrt(spread + 1e-05) * gain


def dot(a, b):
    return jnp.dot(a, b, preferred_element_type=F32)


def block(state, key_mask, query_mask, w_qkv, w_proj, w_up, w_down, gain0, gain1):
    width = state.shape[0]
    depth = width // HEADS
    normed = norm_columns(state, gain0).astype(BF16)
    qkv = dot(w_qkv, normed)
    scale = depth ** (-0.5) * np.log2(np.e)
    query = (qkv[:width] * scale).astype(BF16)
    keys = qkv[width : 2 * width].astype(BF16)
    vals = qkv[2 * width :].astype(BF16)
    ones = jnp.ones((16, LANES), BF16)
    mixed = []
    for head in range(HEADS):
        rows = slice(head * depth, (head + 1) * depth)
        q = jnp.concatenate([query[rows], query_mask], 0)
        k = jnp.concatenate([keys[rows], key_mask], 0)
        scores = lax.dot_general(k, q, (((0,), (0,)), ((), ())), preferred_element_type=F32)
        top = jnp.max(scores, 0, keepdims=True)
        weights = jnp.exp2(scores - top).astype(BF16)
        both = dot(jnp.concatenate([vals[rows], ones], 0), weights)
        mixed.append(both[:depth] / both[depth : depth + 1])
    mixed = jnp.concatenate(mixed, 0).astype(BF16)
    state = (state + dot(w_proj, mixed)).astype(BF16).astype(F32)
    normed = norm_columns(state, gain1).astype(BF16)
    upper = jax.nn.gelu(dot(w_up, normed)).astype(BF16)
    return (state + dot(w_down, upper)).astype(BF16)


def kernel(
    sizes, facts_in, vol_in, wqkv_in, wproj_in, wup_in, tdown_in, gain_in, cw_in, cg_in,
    out_ref, facts_ref, vol_ref, wqkv_ref, wproj_ref, wup_ref, tdown, gain_ref, cw_ref, cg_ref,
    wide, win, r1, r2, tqkv, tproj, tup, tgain, rows_s, pad, cols, cw, ys,
    send1, recv1, send2, recv2, loaded,
):
    pairs = (
        (vol_in, vol_ref), (wqkv_in, wqkv_ref), (wproj_in, wproj_ref), (wup_in, wup_ref),
        (gain_in, gain_ref), (tdown_in, tdown), (facts_in, facts_ref), (cg_in, cg_ref),
        (cw_in, cw_ref),
    )
    loads = [pltpu.make_async_copy(a, b, loaded.at[i]) for i, (a, b) in enumerate(pairs)]
    for load in loads:
        load.start()

    sx, sy, sz, width = sizes
    nwin = sz // WINDOW
    axes = ("gx", "gy", "gz")
    here = [lax.axis_index(a) for a in axes]
    count = [lax.axis_size(a) for a in axes]

    def device(steps, sign):
        return {
            a: lax.rem(here[i] + sign * steps[i] + count[i], count[i]) for i, a in enumerate(axes)
        }

    others = [s for s in itertools.product((0, 1), repeat=3) if any(s)]
    barrier = pltpu.get_barrier_semaphore()
    for steps in others:
        for sign in (-1, 1):
            pl.semaphore_signal(barrier, inc=1, device_id=device(steps, sign), device_id_type=MESH)

    for load in loads[1:8]:
        load.wait()
    for b in range(2):
        tqkv[b] = wqkv_ref[b].astype(F32).T.astype(BF16)
        tproj[b] = wproj_ref[b].astype(F32).T.astype(BF16)
        tup[b] = wup_ref[b].astype(F32).T.astype(BF16)
        for i in range(2):
            wide_gain = jnp.broadcast_to(gain_ref[b, i : i + 1, :], (LANE, width)).T
            tgain[b, i] = jnp.concatenate([wide_gain] * TILES, 1)
    win[...] = jnp.zeros_like(win)
    loads[0].wait()
    wide[:, :sz, :] = vol_ref[...].reshape(sx * sy, sz, width).astype(F32)

    def gather(w, carry):
        for (x, y), lane in PLACE.items():
            win[w, pl.ds(lane, WINDOW), :] = wide[x * sy + y, pl.ds(w * WINDOW, WINDOW), :]
        return carry

    lax.fori_loop(0, nwin, gather, 0)

    xlow, ylow, zlow, valid = [facts_ref[i : i + 1, :] for i in range(4)]
    last = [jnp.where(here[i] == count[i] - 1, 1, 0) for i in range(3)]
    row = lax.broadcasted_iota(jnp.int32, (16, LANES), 0)

    def masks(code):
        key = jnp.where(row == 8, 1 - valid, jnp.where(row == code, valid, 0))
        query = jnp.where(row == code, 0.0, jnp.where(row <= 8, -1e30, 0.0))
        return key.astype(F32).astype(BF16), query.astype(BF16)

    def labels(w):
        edge = last[2] * jnp.where(w == nwin - 1, 1, 0)
        return masks(4 * last[0] * xlow + 2 * last[1] * ylow + edge * zlow)

    def weights(b):
        return tqkv[b], tproj[b], tup[b], tdown[b], tgain[b, 0], tgain[b, 1]

    def put(ref, at, value):
        for tile in range(TILES):
            ref[0, at, tile] = value[:, tile * LANE : (tile + 1) * LANE]

    spans = {0: (0, 1), 1: (1, 1), 2: (2, 1), 3: (1, 2)}

    def copies1(w, across):
        found = []
        for source in range(0 if across else 1, 4):
            start, size = spans[source]
            steps = (source % 2, source // 2, 1 if across else 0)
            sem = 3 * nwin + source if across else 3 * w + source - 1
            found.append(
                pltpu.make_async_remote_copy(
                    src_ref=r1.at[0, w, pl.ds(start, size)],
                    dst_ref=r1.at[source, nwin if across else w, pl.ds(start, size)],
                    send_sem=send1.at[sem],
                    recv_sem=recv1.at[sem],
                    device_id=device(steps, -1),
                    device_id_type=MESH,
                )
            )
        return found

    def copies2(w, across):
        found = []
        for source in range(0 if across else 1, 4):
            steps = (source % 2, source // 2, 1 if across else 0)
            sem = 3 * nwin + source if across else 3 * w + source - 1
            found.append(
                pltpu.make_async_remote_copy(
                    src_ref=r2.at[0, w + 1],
                    dst_ref=r2.at[source, 0 if across else w + 1],
                    send_sem=send2.at[sem],
                    recv_sem=recv2.at[sem],
                    device_id=device(steps, 1),
                    device_id_type=MESH,
                )
            )
        return found

    plain_key, plain_query = masks(jnp.zeros((1, LANES), jnp.int32))

    def first(i, carry):
        pair = [lax.rem(2 * i + at + nwin - 1, nwin) for at in range(2)]
        outs = [block(win[w].T, plain_key, plain_query, *weights(0)) for w in pair]
        for w, out in zip(pair, outs):
            put(r1, w, out)

        @pl.when(i == 0)
        def _():
            pl.semaphore_wait(barrier, 2 * len(others))

        for w in pair:
            for copy in copies1(w, False):
                copy.start()

        @pl.when(i == 0)
        def _():
            for copy in copies1(0, True):
                copy.start()

        return carry

    lax.fori_loop(0, nwin // 2, first, 0)

    def natural1(j):
        both = (xlow * ylow) == 1
        one = both[:, LANE : 2 * LANE]
        two = both[:, 2 * LANE :]
        return jnp.concatenate(
            [
                r1[0, j, 0].astype(F32),
                jnp.where(one, r1[3, j, 1].astype(F32), r1[1, j, 1].astype(F32)),
                jnp.where(two, r1[3, j, 2].astype(F32), r1[2, j, 2].astype(F32)),
            ],
            1,
        )

    def second(i, carry):
        w = lax.rem(i + nwin - 1, nwin)

        @pl.when(i == 0)
        def _():
            for copy in copies1(nwin - 1, False) + copies1(0, True):
                copy.wait()

        @pl.when(i == 1)
        def _():
            for copy in copies1(0, False):
                copy.wait()

        @pl.when((i > 0) & (i < nwin - 1))
        def _():
            for copy in copies1(i, False):
                copy.wait()

        state = jnp.where(zlow == 1, natural1(w + 1), natural1(w))
        key_mask, query_mask = labels(w)
        out = block(state, key_mask, query_mask, *weights(1))
        put(r2, w + 1, out)
        for copy in copies2(w, False):
            copy.start()

        @pl.when(w == nwin - 1)
        def _():
            for copy in copies2(nwin - 1, True):
                copy.start()

        return carry

    lax.fori_loop(0, nwin, second, 0)

    loads[8].wait()
    for dy in range(3):
        for dz in range(3):
            cw[dy, dz * width : (dz + 1) * width, :] = jnp.concatenate(
                [cw_ref[9 * dx + 3 * dy + dz].astype(F32) for dx in range(3)], 1
            ).astype(BF16)

    py = sy + 2

    def spread(jj, partial):
        low_at = lax.rem(jj + nwin, nwin + 1)
        high_at = jnp.where(partial, low_at, lax.rem(jj, nwin + 1))
        outer = jnp.where((jj == 0) | (jj == nwin + 1), 1, 0)
        above = jnp.where(here[2] < count[2] - 1, 1, 0)
        below = jnp.where(here[2] > 0, 1, 0)
        keep = jnp.where(zlow == 1, jnp.maximum(above, 1 - outer), jnp.maximum(below, 1 - outer))
        for source in range(4):
            tiles = []
            for tile in range(TILES):
                part = slice(tile * LANE, (tile + 1) * LANE)
                value = jnp.where(
                    zlow[:, part] == 1,
                    r2[source, low_at, tile].astype(F32),
                    r2[source, high_at, tile].astype(F32),
                )
                tiles.append(jnp.where(keep[:, part] == 1, value, 0.0))
            rows_s[source] = jnp.concatenate(tiles, 1).T
        for x in range(-1, sx + 1):
            for y in range(-1, sy + 1):
                ok = None
                fromx = x < SHIFT
                fromy = y < SHIFT
                for at, axis, size in ((x, 0, sx), (y, 1, sy)):
                    if at == -1:
                        test = here[axis] > 0
                    elif at == size:
                        test = here[axis] < count[axis] - 1
                    else:
                        continue
                    ok = test if ok is None else ok & test
                source = int(fromx) + 2 * int(fromy)
                lane = PLACE[x % WINDOW, y % WINDOW]
                value = rows_s[source, pl.ds(lane, WINDOW), :]
                if ok is not None:
                    value = jnp.where(ok, value, 0.0)
                pad[(x + 1) * py + y + 1, pl.ds(1 + WINDOW * jj, WINDOW), :] = value

    deep = cols.shape[1]

    def convolve(chunk):
        base = WINDOW + chunk * deep

        def stack(xp, carry):
            for y in range(py):
                at = xp * py + y
                cols[at] = jnp.concatenate(
                    [pad[at, base + dz : base + dz + deep, :] for dz in range(3)], 1
                ).astype(BF16)
            total = None
            for dy in range(3):
                piece = cols[pl.ds(xp * py + dy, sy)].reshape(sy * deep, 3 * width)
                part = dot(piece, cw[dy])
                total = part if total is None else total + part
            ys[xp] = total
            return carry

        lax.fori_loop(0, sx + 2, stack, 0, unroll=True)
        size = min(deep, sz - chunk * deep)

        def finish(x, carry):
            total = (
                ys[x][:, :width]
                + ys[x + 1][:, width : 2 * width]
                + ys[x + 2][:, 2 * width : 3 * width]
            )
            value = norm_rows(total, cg_ref[...])
            value = jnp.where(value >= 0, value, 0.01 * value).reshape(sy, deep, width)
            centre = pad[pl.ds((x + 1) * py + 1, sy), base + 1 : base + 1 + deep, :]
            out_ref[x, :, chunk * deep : chunk * deep + size, :] = (centre + value)[
                :, :size
            ].astype(BF16)
            return carry

        lax.fori_loop(0, sx, finish, 0, unroll=True)

    for w in range(nwin):
        if w != nwin - 2:
            for copy in copies2(w, False):
                copy.wait()
    for copy in copies2(nwin - 1, True):
        copy.wait()

    def spread_early(i, carry):
        spread(lax.rem(i + nwin + 1, nwin + 2), i == nwin)
        return carry

    def spread_late(i, carry):
        spread(i, False)
        return carry

    lax.fori_loop(0, nwin + 1, spread_early, 0)
    chunks = -(-sz // deep)
    early = sum(deep * (c + 1) < WINDOW * (nwin - 2) + SHIFT for c in range(chunks))
    for c in range(early):
        convolve(c)
    for copy in copies2(nwin - 2, False):
        copy.wait()
    lax.fori_loop(nwin - 1, nwin + 1, spread_late, 0)
    for c in range(early, chunks):
        convolve(c)


def body(volume, w_qkv, w_proj, w_up, w_down, norm_gain, conv_weight, conv_gain):
    sx, sy, sz, width = volume.shape
    assert sx == WINDOW and sy == WINDOW and sz % (2 * WINDOW) == 0
    nwin = sz // WINDOW
    hidden = w_up.shape[-1]
    deep = -(-sz // 16) * 16
    tall = -(-(WINDOW + 2 + max(deep, sz + WINDOW)) // 8) * 8
    ncopy = 3 * nwin + 4
    padded = (sx + 2) * (sy + 2)
    vmem = pl.BlockSpec(memory_space=pltpu.VMEM)
    sems = [pltpu.SemaphoreType.DMA((ncopy,))] * 4
    operands = (
        jnp.asarray(lane_facts()), volume, w_qkv, w_proj, w_up, jnp.swapaxes(w_down, 1, 2),
        norm_gain, conv_weight, conv_gain.reshape(1, width),
    )
    return pl.pallas_call(
        functools.partial(kernel, (sx, sy, sz, width)),
        out_shape=jax.ShapeDtypeStruct(volume.shape, BF16),
        in_specs=[pl.BlockSpec(memory_space=pltpu.HBM)] * 9,
        out_specs=vmem,
        scratch_shapes=[pltpu.VMEM(o.shape, o.dtype) for o in operands]
        + [
            pltpu.VMEM((sx * sy, deep, width), F32),
            pltpu.VMEM((nwin, LANES, width), F32),
            pltpu.VMEM((4, nwin + 1, TILES, width, LANE), BF16),
            pltpu.VMEM((4, nwin + 1, TILES, width, LANE), BF16),
            pltpu.VMEM((2, 3 * width, width), BF16),
            pltpu.VMEM((2, width, width), BF16),
            pltpu.VMEM((2, hidden, width), BF16),
            pltpu.VMEM((2, 2, width, LANES), F32),
            pltpu.VMEM((4, LANES, width), F32),
            pltpu.VMEM((padded, tall, width), F32),
            pltpu.VMEM((padded, 16, 3 * width), BF16),
            pltpu.VMEM((3, 3 * width, 3 * width), BF16),
            pltpu.VMEM((sx + 2, sy * 16, 3 * width), F32),
        ]
        + sems
        + [pltpu.SemaphoreType.DMA((9,))],
        compiler_params=pltpu.CompilerParams(
            collective_id=0, has_side_effects=True, vmem_limit_bytes=64 * 1024 * 1024 - 65536
        ),
    )(*operands)


def solution(mesh):
    placed = (P(("parts", "gx"), "gy", "gz", None), P(), P(), P(), P(), P(), P(), P())
    return jax.shard_map(
        body,
        mesh=mesh,
        in_specs=placed,
        out_specs=P(("parts", "gx"), "gy", "gz", None),
        check_vma=False,
    )
```
